512 devices in a mesh: fsdp: 32 (over z_lo, x), dp: 16 (over z_hi, y, core).
Axes of the slice: x: 4, y: 4, z: 16 (z_hi: 2, z_lo: 8; z = z_hi * 8 + z_lo), core: 2. Of those that a mesh axis runs over, the one named last changes fastest.
Arguments:
- tokens: bfloat16 [12288, 4096], P(('dp', 'fsdp')), parts along dimension 0, may hold values from -6 to 6
- frozen_slot_rows: bfloat16 [73728, 14336], P(('dp', 'fsdp')), parts along dimension 0
- adapter_down_factor: bfloat16 [73728, 64], P(('dp', 'fsdp')), parts along dimension 0, may hold values from -18 to 18
- adapter_up_factor: bfloat16 [1024, 14336], P('dp', 'fsdp'), parts along dimension 0, may hold values from -0.046875 to 0.046875
- magnitude: bfloat16 [229376], P(('dp', 'fsdp')), parts along dimension 0, may hold values from 0.5 to 2
- counts: int32 [512], P('dp'), parts along dimension 0, may hold values from 1 to 144, 4096 in all
Outputs:
- projected: bfloat16 [12288, 14336], P('dp', 'fsdp'), parts along dimension 0
The draws below stay inside these ranges and needn't reach their ends.
There are 16 independent parts, one for each index of `dp`. The reference program is written for one: setup_inputs(seed, part) draws one part's arguments, and reference() takes and returns one part's arrays. A program takes and returns all parts, laid end to end along the dimension named above; each array names one. Nothing has to cross between parts.
Inputs may be any that keep to these rules, and one draw needn't show every extreme that they name: counts are at least 1, sum to 4096, and the largest equals 144; slots at or beyond a device's count hold arbitrary values.
All inputs are finite; a program needn't handle non-finite values.
Results may differ from the reference program's by a relative error of at most 0.0049.
Values may be sent and summed in bfloat16 or wider, within the bound.
No kernel may reach another device: no remote copies, remote signals or barrier semaphores. Data moves between devices by JAX's collectives and lax.ppermute only.
A program may use at most 64 MiB of HBM per device.

```python
import math
import jax
import jax.numpy as jnp
import numpy as np
from jax import lax

INPUT_FEATURES = 4096
HIDDEN_UNITS = 14336
LOW_RANK_SIZE = 64
SLOT_ROWS = 144
TOKENS = 768
N_FSDP = 32


def draw_frozen_slot_rows(key, part):
    key = jax.random.fold_in(key, 11)
    keys = jax.random.split(key, 3)
    total = N_FSDP * SLOT_ROWS
    owner = (jnp.arange(total) // SLOT_ROWS).astype(jnp.float32)[:, None]
    row_level = 0.5 * owner / max(N_FSDP - 1, 1) + 0.5 * jax.random.uniform(keys[0], (total, 1))
    col_level = jax.random.uniform(keys[1], (1, HIDDEN_UNITS))
    noise = jax.random.normal(keys[2], (total, HIDDEN_UNITS))
    scale = jnp.power(10.0, row_level) * jnp.power(10.0, col_level) * INPUT_FEATURES ** (-0.5)
    return (noise * scale).astype(jnp.float32).astype(jnp.bfloat16)


def block_levels(stream_key, shape, shards, least, high):
    level, own = 1.0, jax.random.fold_in(stream_key, 6)
    for position, parts in shards:
        heights = jnp.exp(jax.random.uniform(jax.random.fold_in(own, position), (parts,), jnp.float32, least / len(shards), high / len(shards)))
        level = level * jnp.repeat(heights, shape[position] // parts).reshape([-1 if axis == position else 1 for axis in range(len(shape))])
    return level


def split_up(number_of, total, bound, slope):
    loads = [(1 << 20) // math.isqrt(rank ** slope) + 1 for rank in range(2, number_of + 1)]
    rest, given = total - bound - (number_of - 1), [1] * (number_of - 1)
    while rest > 0:
        movable = [i for i in range(number_of - 1) if given[i] < bound]
        mass, remaining = sum([loads[i] for i in movable]), rest
        for i in movable:
            more = min(bound - given[i], max(1, remaining * loads[i] // mass), rest)
            given[i] = given[i] + more
            rest = rest - more
    return np.array([bound] + given)


def ragged(own_key, number_of, total, bound, lean):
    if number_of == 2:
        one = jax.random.randint(own_key, (), max(1, total - bound), min(bound, total - 1) + 1)
        return jnp.stack([one, total - one])
    sizes = jnp.asarray(split_up(number_of, total, bound, lean), jnp.int32)
    couples = (number_of - 1) // 2
    giver, sink = sizes[1:1 + 2 * couples:2], sizes[2:2 + 2 * couples:2]
    margin = jnp.minimum(giver - 1, bound - sink)
    passed = jax.random.randint(jax.random.fold_in(own_key, 1), (couples,), 0, 1 << 20) % (margin + 1)
    sizes = sizes.at[1:1 + 2 * couples:2].set(giver - passed).at[2:2 + 2 * couples:2].set(sink + passed)
    return sizes[jax.random.permutation(jax.random.fold_in(own_key, 2), number_of)]


def centred(stream_key, dims, scale, bound, shards=(), kind=jnp.bfloat16):
    factor_of = block_levels(stream_key, dims, shards, -0.22, 0.18) if shards else 1.0
    values = jax.random.normal(stream_key, dims, jnp.float32) * scale * factor_of
    return jnp.minimum(jnp.maximum(values, -bound), bound).astype(kind)


def setup_inputs(seed: int = 0, part: int = 0) -> dict:
    key_list = jax.random.split(jax.random.key(seed), 7)
    own_keys = jax.random.split(jax.random.fold_in(key_list[6], part), 7)
    tokens = centred(own_keys[0], (TOKENS, INPUT_FEATURES), 1.0, 6.0, ((0, 32),))
    frozen_slot_rows = draw_frozen_slot_rows(jax.random.fold_in(jax.random.fold_in(key_list[6], part), 71), part)
    adapter_down_factor = centred(own_keys[2], (N_FSDP * SLOT_ROWS, LOW_RANK_SIZE), 3.0, 18.0, ((0, 32),))
    adapter_up_factor = centred(own_keys[3], (LOW_RANK_SIZE, HIDDEN_UNITS), (INPUT_FEATURES * LOW_RANK_SIZE // 16) ** -0.5, 0.046875, ((1, 32),))
    magnitude = jnp.clip(jnp.exp(math.log(2.0) - 1.3862944 * jax.random.uniform(own_keys[4], (HIDDEN_UNITS,), jnp.float32) ** block_levels(own_keys[4], (HIDDEN_UNITS,), ((0, 32),), -0.2, 0.2)), 0.5, 2.0).astype(jnp.bfloat16)
    counts = ragged(own_keys[5], N_FSDP, INPUT_FEATURES, SLOT_ROWS, 2).astype(jnp.int32)
    return {"tokens": tokens, "frozen_slot_rows": frozen_slot_rows, "adapter_down_factor": adapter_down_factor, "adapter_up_factor": adapter_up_factor, "magnitude": magnitude, "counts": counts}


def locate(counts, slots_per, total_rows):
    offsets = jnp.cumsum(counts).astype(jnp.int32) - counts
    row_ids = jnp.arange(total_rows, dtype=jnp.int32)
    owner = lax.optimization_barrier(jnp.sum((offsets[None, :] <= row_ids[:, None]).astype(jnp.int32), axis=1)) - 1
    picked = jnp.arange(counts.shape[0], dtype=jnp.int32)[None, :] == owner[:, None]
    first = lax.optimization_barrier(jnp.sum(jnp.where(picked, offsets[None, :], 0), axis=1)).astype(jnp.int32)
    return (owner * slots_per + row_ids - first).astype(jnp.int32)

def reference(tokens, frozen_slot_rows, adapter_down_factor, adapter_up_factor, magnitude, counts):
    slot_positions = locate(counts, frozen_slot_rows.shape[0] // counts.shape[0], tokens.shape[1])
    base_matrix = jnp.take(frozen_slot_rows, slot_positions, axis=0)
    down_factor = jnp.take(adapter_down_factor, slot_positions, axis=0)
    merged_weight = base_matrix.astype(jnp.float32) + jnp.dot(down_factor, adapter_up_factor, preferred_element_type=jnp.float32)
    col_norm = jnp.sqrt(lax.optimization_barrier(jnp.sum(merged_weight * merged_weight, axis=0)) + 1e-06)
    scaled = (magnitude.astype(jnp.float32) * merged_weight / col_norm).astype(jnp.bfloat16)
    return jnp.dot(tokens, scaled, preferred_element_type=jnp.float32).astype(jnp.bfloat16)
```

```python
import functools

import jax
import jax.numpy as jnp
from jax import lax
from jax.experimental import pallas as pl
from jax.experimental.pallas import tpu as pltpu
from jax.sharding import PartitionSpec as P

AXIS = "fsdp"
GROUP = 8
PAIRS = 4
SLOTS = 144
RANK = 64
UNITS = 448
KEYS = GROUP * SLOTS
TOKENS = 768
OWN_TOKENS = 24
FEATURES = 4096
WINDOW = 384
CHUNKS = ((0, 256), (256, 192))
VMEM_LIMIT = 48 * 1024 * 1024

NEAR = [[GROUP * p + i for i in range(GROUP)] for p in range(PAIRS)]
FAR = [[GROUP * p + i for p in range(PAIRS)] for i in range(GROUP)]
ALONG_X = [[4 * z + x for x in range(4)] for z in range(8)]


def whole(memory_space=pltpu.VMEM):
    return pl.BlockSpec(memory_space=memory_space)


def params():
    return pltpu.CompilerParams(vmem_limit_bytes=VMEM_LIMIT)


def window_kernel(place_ref, counts_ref, tokens_ref, out_ref, padded, lined):
    padded[:, FEATURES:] = jnp.zeros((OWN_TOKENS, WINDOW), jnp.float32)
    padded[:, :FEATURES] = tokens_ref[...].astype(jnp.float32)
    starts = [jnp.int32(0)]
    for f in range(GROUP * PAIRS - 1):
        starts.append(starts[-1] + counts_ref[f])
    pair = place_ref[0] // GROUP
    lane = lax.broadcasted_iota(jnp.int32, (OWN_TOKENS, WINDOW), 1)
    for target in range(PAIRS):
        for i in range(GROUP):
            start = starts[GROUP * target + i]
            base = pl.multiple_of((start // 128) * 128, 128)
            place = SLOTS * i
            low = (place // 128) * 128
            rest = place - low
            shift = lax.rem(rest - (start - base) + WINDOW, WINDOW)
            moved = pltpu.roll(padded[:, pl.ds(base, WINDOW)], shift, 1)
            keep = (lane >= rest) & (lane < rest + SLOTS)
            lined[:, low : low + WINDOW] = jnp.where(keep, moved, lined[:, low : low + WINDOW])
        out_ref[lax.rem(target - pair + PAIRS, PAIRS)] = lined[:, :KEYS].astype(jnp.bfloat16)


def own_windows(place, counts, tokens):
    return pl.pallas_call(
        window_kernel,
        out_shape=jax.ShapeDtypeStruct((PAIRS, OWN_TOKENS, KEYS), jnp.bfloat16),
        in_specs=[whole(pltpu.SMEM), whole(pltpu.SMEM), whole()],
        out_specs=whole(),
        scratch_shapes=[
            pltpu.VMEM((OWN_TOKENS, FEATURES + WINDOW), jnp.float32),
            pltpu.VMEM((OWN_TOKENS, KEYS + 128), jnp.float32),
        ],
        compiler_params=params(),
    )(place, counts, tokens)


def collect_kernel(place_ref, own_ref, one_ref, two_ref, three_ref, down_ref, out_ref, rows):
    pair = place_ref[0] // GROUP
    blocks = (own_ref[0], one_ref[...], two_ref[...], three_ref[...])
    for step, block in enumerate(blocks):
        origin = lax.rem(pair - step + PAIRS, PAIRS)
        rows[pl.ds(pl.multiple_of(origin * OWN_TOKENS, 8), OWN_TOKENS), :] = block.astype(jnp.float32)
    down = down_ref[...].astype(jnp.float32)
    rows[PAIRS * OWN_TOKENS :, :] = jnp.concatenate(
        [down[8 * g : 8 * g + 8, :] for g in range(SLOTS // 8)], axis=1
    )
    out_ref[...] = rows[...].astype(jnp.bfloat16)


def collect(place, own, one, two, three, down):
    height = PAIRS * OWN_TOKENS + 8
    return pl.pallas_call(
        collect_kernel,
        out_shape=jax.ShapeDtypeStruct((height, KEYS), jnp.bfloat16),
        in_specs=[whole(pltpu.SMEM)] + [whole()] * 5,
        out_specs=whole(),
        scratch_shapes=[pltpu.VMEM((height, KEYS), jnp.float32)],
        compiler_params=params(),
    )(place, own, one, two, three, down)


def pack_kernel(rows_ref, *out_refs):
    step = pl.program_id(0)
    for q in range(PAIRS):

        @pl.when(step == q)
        def _():
            for out_ref, (first, width) in zip(out_refs, CHUNKS):
                for i in range(GROUP):
                    begin = UNITS * i + first
                    out_ref[i, :, q * width : (q + 1) * width] = rows_ref[:, begin : begin + width]


def pack(rows):
    return pl.pallas_call(
        pack_kernel,
        grid=(PAIRS,),
        out_shape=[
            jax.ShapeDtypeStruct((GROUP, SLOTS, PAIRS * width), jnp.bfloat16) for _, width in CHUNKS
        ],
        in_specs=[pl.BlockSpec((SLOTS, GROUP * UNITS), lambda q: (0, q))],
        out_specs=[
            pl.BlockSpec((GROUP, SLOTS, PAIRS * width), lambda q: (0, 0, 0)) for _, width in CHUNKS
        ],
        compiler_params=params(),
    )(rows)


def partial_kernel(first, width, place_ref, counts_ref, rows_ref, blocks_ref, up0_ref, up1_ref, up2_ref, up3_ref, out_ref, squares_ref, tokens, merged, ups):
    place = place_ref[0]
    pair, side = place // GROUP, (place // 4) % 2
    row = lax.broadcasted_iota(jnp.int32, (SLOTS, width), 0)
    downs, valid = [], []
    for i in range(GROUP):
        origin = lax.rem(side + i // 4, 2)
        tokens[96 * i : 96 * i + 96, :] = blocks_ref[i % 4, origin, 0:96, :]
        folded = blocks_ref[i % 4, origin, 96:104, :].astype(jnp.float32)
        downs.append(
            jnp.concatenate([folded[:, RANK * g : RANK * g + RANK] for g in range(SLOTS // 8)], axis=0).astype(jnp.bfloat16)
        )
        valid.append(row < counts_ref[GROUP * pair + i])
    for step, up_ref in enumerate((up0_ref, up1_ref, up2_ref, up3_ref)):
        ups[lax.rem(pair - step + PAIRS, PAIRS)] = up_ref[...]
    all_tokens = tokens[...]
    for q in range(PAIRS):
        up = ups[q, :, first : first + width]
        total = jnp.zeros((1, width), jnp.float32)
        for i in range(GROUP):
            low = jnp.dot(downs[i], up, preferred_element_type=jnp.float32)
            base = rows_ref[i, :, q * width : (q + 1) * width].astype(jnp.float32)
            value = jnp.where(valid[i], base + low, 0.0)
            total = total + jnp.sum(value * value, axis=0, keepdims=True)
            merged[SLOTS * i : SLOTS * i + SLOTS, :] = value.astype(jnp.bfloat16)
        squares_ref[q] = total
        out_ref[q] = lax.dot_general(
            merged[...], all_tokens, (((0,), (1,)), ((), ())), preferred_element_type=jnp.float32
        ).astype(jnp.bfloat16)


def partial_products(chunk, place, counts, rows, blocks, ups):
    first, width = chunk
    return pl.pallas_call(
        functools.partial(partial_kernel, first, width),
        out_shape=[
            jax.ShapeDtypeStruct((PAIRS, width, TOKENS), jnp.bfloat16),
            jax.ShapeDtypeStruct((PAIRS, 1, width), jnp.float32),
        ],
        in_specs=[whole(pltpu.SMEM), whole(pltpu.SMEM)] + [whole()] * 6,
        out_specs=[whole(), whole()],
        scratch_shapes=[
            pltpu.VMEM((TOKENS, KEYS), jnp.bfloat16),
            pltpu.VMEM((KEYS, width), jnp.bfloat16),
            pltpu.VMEM((PAIRS, RANK, UNITS), jnp.bfloat16),
        ],
        compiler_params=params(),
    )(place, counts, rows, blocks, *ups)


def finish_kernel(squares_ref, scale_ref, *refs):
    sum_refs, out_ref = refs[:-1], refs[-1]
    total = jnp.sum(squares_ref[...], axis=0)
    factor = scale_ref[...].astype(jnp.float32) / jnp.sqrt(total + 1e-06)
    sums = jnp.concatenate([s[...].astype(jnp.float32) for s in sum_refs], axis=0).T
    result = jnp.where(factor == 0.0, 0.0, sums * factor)
    out_ref[...] = jnp.concatenate(
        [
            result[OWN_TOKENS * (PAIRS * i + q) : OWN_TOKENS * (PAIRS * i + q + 1), :]
            for q in range(PAIRS)
            for i in range(GROUP)
        ],
        axis=0,
    ).astype(jnp.bfloat16)


def finish(squares, scale, sums):
    return pl.pallas_call(
        finish_kernel,
        out_shape=jax.ShapeDtypeStruct((TOKENS, UNITS), jnp.bfloat16),
        in_specs=[whole()] * (2 + len(sums)),
        out_specs=whole(),
        compiler_params=params(),
    )(squares, scale, *sums)


def to_pair(array, step):
    return lax.ppermute(
        array,
        AXIS,
        [(GROUP * p + i, GROUP * ((p + step) % PAIRS) + i) for p in range(PAIRS) for i in range(GROUP)],
    )


def body(tokens, frozen_slot_rows, adapter_down_factor, adapter_up_factor, magnitude, counts):
    place = lax.axis_index(AXIS).astype(jnp.int32).reshape(1)
    own = own_windows(place, counts, tokens)
    moved = [to_pair(own[step], step) for step in range(1, PAIRS)]
    ups = [adapter_up_factor] + [to_pair(adapter_up_factor, step) for step in range(1, PAIRS)]
    column = collect(place, own, *moved, adapter_down_factor)
    other = lax.ppermute(column, AXIS, [(f, f ^ 4) for f in range(GROUP * PAIRS)])
    pair_blocks = jnp.stack([column, other])
    packed = list(pack(frozen_slot_rows))
    packed[0], pair_blocks = lax.optimization_barrier((packed[0], pair_blocks))
    blocks = lax.all_gather(pair_blocks, AXIS, axis_index_groups=ALONG_X, axis=0)
    sums, squares = [], []
    product = None
    for chunk, send in zip(CHUNKS, packed):
        if product is not None:
            send, product = lax.optimization_barrier((send, product))
            sums.append(lax.psum_scatter(product, AXIS, axis_index_groups=FAR, scatter_dimension=0, tiled=False))
        rows = lax.all_to_all(send, AXIS, 0, 0, axis_index_groups=NEAR, tiled=True)
        product, square = partial_products(chunk, place, counts, rows, blocks, ups)
        squares.append(square)
    sums.append(lax.psum_scatter(product, AXIS, axis_index_groups=FAR, scatter_dimension=0, tiled=False))
    squares = lax.all_to_all(jnp.concatenate(squares, axis=2), AXIS, 0, 0, axis_index_groups=FAR, tiled=True)
    return finish(squares, magnitude.reshape(1, UNITS), sums)


def solution(mesh):
    in_specs = (
        P(("dp", "fsdp"), None),
        P(("dp", "fsdp"), None),
        P(("dp", "fsdp"), None),
        P("dp", "fsdp"),
        P(("dp", "fsdp")),
        P("dp"),
    )
    out_specs = P("dp", "fsdp")
    return jax.shard_map(body, mesh=mesh, in_specs=in_specs, out_specs=out_specs, check_vma=False)
```

```python
import functools

import jax
import jax.numpy as jnp
from jax import lax
from jax.experimental import pallas as pl
from jax.experimental.pallas import tpu as pltpu
from jax.sharding import PartitionSpec as P

AXIS = "fsdp"
GROUP = 8
PAIRS = 4
SLOTS = 144
RANK = 64
UNITS = 448
KEYS = GROUP * SLOTS
TOKENS = 768
OWN_TOKENS = 24
FEATURES = 4096
WINDOW = 384
CHUNKS = ((0, 256), (256, 192))
HALF = TOKENS // 2
TAIL = 16
LANES = 384
VMEM_LIMIT = 48 * 1024 * 1024

NEAR = [[GROUP * p + i for i in range(GROUP)] for p in range(PAIRS)]
FAR = [[GROUP * p + i for p in range(PAIRS)] for i in range(GROUP)]


def whole(memory_space=pltpu.VMEM):
    return pl.BlockSpec(memory_space=memory_space)


def params():
    return pltpu.CompilerParams(vmem_limit_bytes=VMEM_LIMIT)


def window_kernel(place_ref, counts_ref, tokens_ref, out_ref, padded, lined):
    padded[:, FEATURES:] = jnp.zeros((OWN_TOKENS, WINDOW), jnp.float32)
    padded[:, :FEATURES] = tokens_ref[...].astype(jnp.float32)
    starts = [jnp.int32(0)]
    for f in range(GROUP * PAIRS - 1):
        starts.append(starts[-1] + counts_ref[f])
    pair = place_ref[0] // GROUP
    lane = lax.broadcasted_iota(jnp.int32, (OWN_TOKENS, WINDOW), 1)
    for target in range(PAIRS):
        for i in range(GROUP):
            start = starts[GROUP * target + i]
            base = pl.multiple_of((start // 128) * 128, 128)
            place = SLOTS * i
            low = (place // 128) * 128
            rest = place - low
            shift = lax.rem(rest - (start - base) + WINDOW, WINDOW)
            moved = pltpu.roll(padded[:, pl.ds(base, WINDOW)], shift, 1)
            keep = (lane >= rest) & (lane < rest + SLOTS)
            lined[:, low : low + WINDOW] = jnp.where(keep, moved, lined[:, low : low + WINDOW])
        out_ref[lax.rem(target - pair + PAIRS, PAIRS)] = lined[:, :KEYS].astype(jnp.bfloat16)


def own_windows(place, counts, tokens):
    return pl.pallas_call(
        window_kernel,
        out_shape=jax.ShapeDtypeStruct((PAIRS, OWN_TOKENS, KEYS), jnp.bfloat16),
        in_specs=[whole(pltpu.SMEM), whole(pltpu.SMEM), whole()],
        out_specs=whole(),
        scratch_shapes=[
            pltpu.VMEM((OWN_TOKENS, FEATURES + WINDOW), jnp.float32),
            pltpu.VMEM((OWN_TOKENS, KEYS + 128), jnp.float32),
        ],
        compiler_params=params(),
    )(place, counts, tokens)


def collect_kernel(place_ref, own_ref, one_ref, two_ref, three_ref, down_ref, out_ref, rows):
    pair = place_ref[0] // GROUP
    blocks = (own_ref[0], one_ref[...], two_ref[...], three_ref[...])
    for step, block in enumerate(blocks):
        origin = lax.rem(pair - step + PAIRS, PAIRS)
        rows[pl.ds(pl.multiple_of(origin * OWN_TOKENS, 8), OWN_TOKENS), :] = block.astype(jnp.float32)
    down = down_ref[...].astype(jnp.float32)
    rows[PAIRS * OWN_TOKENS :, :] = jnp.concatenate(
        [down[8 * g : 8 * g + 8, :] for g in range(SLOTS // 8)], axis=1
    )
    out_ref[...] = rows[...].astype(jnp.bfloat16)


def collect(place, own, one, two, three, down):
    height = PAIRS * OWN_TOKENS + 8
    return pl.pallas_call(
        collect_kernel,
        out_shape=jax.ShapeDtypeStruct((height, KEYS), jnp.bfloat16),
        in_specs=[whole(pltpu.SMEM)] + [whole()] * 5,
        out_specs=whole(),
        scratch_shapes=[pltpu.VMEM((height, KEYS), jnp.float32)],
        compiler_params=params(),
    )(place, own, one, two, three, down)


def pack_kernel(rows_ref, out_ref):
    step = pl.program_id(0)
    for q in range(PAIRS):

        @pl.when(step == q)
        def _():
            for i in range(GROUP):
                out_ref[i, :, UNITS * q : UNITS * (q + 1)] = rows_ref[:, UNITS * i : UNITS * (i + 1)]


def pack(rows):
    return pl.pallas_call(
        pack_kernel,
        grid=(PAIRS,),
        out_shape=jax.ShapeDtypeStruct((GROUP, SLOTS, PAIRS * UNITS), jnp.bfloat16),
        in_specs=[pl.BlockSpec((SLOTS, GROUP * UNITS), lambda q: (0, q))],
        out_specs=pl.BlockSpec((GROUP, SLOTS, PAIRS * UNITS), lambda q: (0, 0, 0)),
        compiler_params=params(),
    )(rows)


def assemble_kernel(place_ref, *refs):
    block_refs, up_refs = refs[:4], refs[4:8]
    tokens_ref, down_ref, up_ref = refs[8:]
    place = place_ref[0]
    pair, side, x = place // GROUP, (place // 4) % 2, place % 4
    for step, block_ref in enumerate(block_refs):
        for far in range(2):
            origin = 4 * lax.rem(side + far, 2) + lax.rem(x - step + 4, 4)
            tokens_ref[pl.ds(pl.multiple_of(origin * 96, 96), 96), :] = block_ref[far, 0:96, :]
            folded = block_ref[far, 96:104, :].astype(jnp.float32)
            down_ref[origin] = jnp.concatenate(
                [folded[:, RANK * g : RANK * g + RANK] for g in range(SLOTS // 8)], axis=0
            ).astype(jnp.bfloat16)
    for step, ref in enumerate(up_refs):
        up_ref[lax.rem(pair - step + PAIRS, PAIRS)] = ref[...]


def assemble(place, blocks, ups):
    return pl.pallas_call(
        assemble_kernel,
        out_shape=[
            jax.ShapeDtypeStruct((TOKENS, KEYS), jnp.bfloat16),
            jax.ShapeDtypeStruct((GROUP, SLOTS, RANK), jnp.bfloat16),
            jax.ShapeDtypeStruct((PAIRS, RANK, UNITS), jnp.bfloat16),
        ],
        in_specs=[whole(pltpu.SMEM)] + [whole()] * 8,
        out_specs=[whole()] * 3,
        compiler_params=params(),
    )(place, *blocks, *ups)


def split(total):
    pieces = [total[:, : UNITS // 2], total[:, UNITS // 2 :]]
    rows = []
    for piece in pieces:
        high = piece.astype(jnp.bfloat16).astype(jnp.float32)
        rows += [high, piece - high]
    rows.append(jnp.zeros((TAIL - 4, UNITS // 2), jnp.float32))
    rows = jnp.concatenate(rows, axis=0)
    return jnp.concatenate([rows, jnp.zeros((TAIL, LANES - UNITS // 2), jnp.float32)], axis=1).astype(jnp.bfloat16)


def joined(tail):
    rows = tail.astype(jnp.float32)[:, : UNITS // 2]
    return jnp.concatenate([rows[0:1] + rows[1:2], rows[2:3] + rows[3:4]], axis=1)


def partial_kernel(chunk, place_ref, counts_ref, rows_ref, tokens_ref, down_ref, up_ref, *refs):
    first, width = chunk
    last = first > 0
    earlier_ref = refs[0] if last else None
    squares_ref, out_ref, above_ref, below_ref, merged = refs[-5:]
    pair = place_ref[0] // GROUP
    row = lax.broadcasted_iota(jnp.int32, (SLOTS, width), 0)
    valid = [row < counts_ref[GROUP * pair + i] for i in range(GROUP)]
    for q in range(PAIRS):
        up = up_ref[q, :, first : first + width]
        total = jnp.zeros((1, width), jnp.float32)
        begin = UNITS * q + first
        for i in range(GROUP):
            low = jnp.dot(down_ref[i], up, preferred_element_type=jnp.float32)
            base = rows_ref[i, :, begin : begin + width].astype(jnp.float32)
            value = jnp.where(valid[i], base + low, 0.0)
            total = total + jnp.sum(value * value, axis=0, keepdims=True)
            merged[SLOTS * i : SLOTS * i + SLOTS, :] = value.astype(jnp.bfloat16)
        product = jnp.dot(tokens_ref[...], merged[...], preferred_element_type=jnp.float32)
        offset = lax.rem(q - pair + PAIRS, PAIRS)
        if last:
            product = jnp.concatenate([product[:HALF], product[HALF:]], axis=1)
            total = jnp.concatenate([earlier_ref[offset], total], axis=1)
        out_ref[offset] = product
        squares_ref[offset] = total

        @pl.when(offset == 3)
        def _():
            above_ref[: product.shape[0]] = product.astype(jnp.bfloat16)
            if last:
                above_ref[HALF:] = split(total)

        @pl.when(offset == 1)
        def _():
            below_ref[: product.shape[0]] = product.astype(jnp.bfloat16)
            if last:
                below_ref[HALF:] = split(total)


def partial_products(chunk, place, counts, rows, tokens, down, up, *earlier):
    width = chunk[1]
    shape = (HALF, 2 * width) if earlier else (TOKENS, width)
    sent = (HALF + TAIL, 2 * width) if earlier else shape
    out_shape = [
        jax.ShapeDtypeStruct((PAIRS, 1, UNITS if earlier else width), jnp.float32),
        jax.ShapeDtypeStruct((PAIRS,) + shape, jnp.float32),
        jax.ShapeDtypeStruct(sent, jnp.bfloat16),
        jax.ShapeDtypeStruct(sent, jnp.bfloat16),
    ]
    return pl.pallas_call(
        functools.partial(partial_kernel, chunk),
        out_shape=out_shape,
        in_specs=[whole(pltpu.SMEM), whole(pltpu.SMEM)] + [whole()] * (4 + len(earlier)),
        out_specs=[whole()] * len(out_shape),
        scratch_shapes=[pltpu.VMEM((KEYS, width), jnp.bfloat16)],
        compiler_params=params(),
    )(place, counts, rows, tokens, down, up, *earlier)


def forward_kernel(up_got_ref, down_got_ref, up_own_ref, down_own_ref, up_squares_ref, down_squares_ref, up_ref, down_ref):
    height = up_own_ref.shape[1]
    for got, own, squares, out in (
        (up_got_ref, up_own_ref, up_squares_ref, up_ref),
        (down_got_ref, down_own_ref, down_squares_ref, down_ref),
    ):
        out[:height] = (got[:height].astype(jnp.float32) + own[0]).astype(jnp.bfloat16)
        if out.shape[0] > height:
            out[height:] = split(joined(got[height:]) + squares[0])


def forward(up_got, down_got, products, squares, step):
    def own(array, offset):
        return pl.BlockSpec((1,) + array.shape[1:], lambda _: (offset, 0, 0))

    got = pl.BlockSpec(up_got.shape, lambda _: (0, 0))
    return pl.pallas_call(
        forward_kernel,
        grid=(1,),
        out_shape=[jax.ShapeDtypeStruct(up_got.shape, jnp.bfloat16)] * 2,
        in_specs=[got, got]
        + [own(products, PAIRS - step), own(products, step), own(squares, PAIRS - step), own(squares, step)],
        out_specs=[got, got],
        compiler_params=params(),
    )(up_got, down_got, products, products, squares, squares)


def finish_kernel(squares_ref, scale_ref, *refs):
    out_ref = refs[-1]
    own, above, below = refs[0:3]
    front = own[0] + above[...].astype(jnp.float32) + below[...].astype(jnp.float32)
    own, above, below = refs[3:6]
    back = own[0] + above[:HALF].astype(jnp.float32) + below[:HALF].astype(jnp.float32)
    width = back.shape[1] // 2
    back = jnp.concatenate([back[:, :width], back[:, width:]], axis=0)
    total = squares_ref[0] + joined(above[HALF:]) + joined(below[HALF:])
    factor = scale_ref[...].astype(jnp.float32) / jnp.sqrt(total + 1e-06)
    result = jnp.concatenate([front, back], axis=1)
    result = jnp.where(factor == 0.0, 0.0, result * factor)
    out_ref[...] = jnp.concatenate(
        [
            result[OWN_TOKENS * (PAIRS * i + q) : OWN_TOKENS * (PAIRS * i + q + 1), :]
            for q in range(PAIRS)
            for i in range(GROUP)
        ],
        axis=0,
    ).astype(jnp.bfloat16)


def finish(squares, scale, sums):
    def same(*shape):
        return pl.BlockSpec(shape, lambda _: (0,) * len(shape))

    return pl.pallas_call(
        finish_kernel,
        grid=(1,),
        out_shape=jax.ShapeDtypeStruct((TOKENS, UNITS), jnp.bfloat16),
        in_specs=[same(1, 1, UNITS), same(1, UNITS)]
        + [same(1, *array.shape[1:]) if array.ndim == 3 else same(*array.shape) for array in sums],
        out_specs=same(TOKENS, UNITS),
        compiler_params=params(),
    )(squares, scale, *sums)


def to_pair(array, step):
    return lax.ppermute(
        array,
        AXIS,
        [(GROUP * p + i, GROUP * ((p + step) % PAIRS) + i) for p in range(PAIRS) for i in range(GROUP)],
    )


def along_x(array, step):
    return lax.ppermute(array, AXIS, [(4 * z + x, 4 * z + (x + step) % 4) for z in range(8) for x in range(4)])


def hop(array, froms, way):
    return lax.ppermute(
        array, AXIS, [(GROUP * p + i, GROUP * (p + way) + i) for p in froms for i in range(GROUP)]
    )


def exchange(send):
    return lax.all_to_all(send, AXIS, 0, 0, axis_index_groups=NEAR, tiled=True)


def hops(sends, step):
    return hop(sends[0], range(step), 1), hop(sends[1], range(PAIRS - step, PAIRS), -1)


def body(tokens, frozen_slot_rows, adapter_down_factor, adapter_up_factor, magnitude, counts):
    place = lax.axis_index(AXIS).astype(jnp.int32).reshape(1)
    send = pack(frozen_slot_rows)
    rows = exchange(send)
    own = own_windows(place, counts, tokens)
    moved = [to_pair(own[step], step) for step in range(1, PAIRS)]
    ups = [adapter_up_factor] + [to_pair(adapter_up_factor, step) for step in range(1, PAIRS)]
    column = collect(place, own, *moved, adapter_down_factor)
    other = lax.ppermute(column, AXIS, [(f, f ^ 4) for f in range(GROUP * PAIRS)])
    blocks = jnp.stack([column, other])
    blocks = [blocks] + [along_x(blocks, step) for step in (1, 3, 2)]
    blocks = [blocks[0], blocks[1], blocks[3], blocks[2]]
    all_tokens, down, up = assemble(place, blocks, ups)
    a_squares, a, *ready = partial_products(CHUNKS[0], place, counts, rows, all_tokens, down, up)
    a_got = hops(ready, 1)
    squares, b, *ready = partial_products(CHUNKS[1], place, counts, rows, all_tokens, down, up, a_squares)
    b_got = hops(ready, 1)
    for step in range(2, PAIRS):
        a_got = hops(forward(*a_got, a, a_squares, step), step)
        b_got = hops(forward(*b_got, b, squares, step), step)
    return finish(squares, magnitude.reshape(1, UNITS), [a, *a_got, b, *b_got])


def solution(mesh):
    in_specs = (
        P(("dp", "fsdp"), None),
        P(("dp", "fsdp"), None),
        P(("dp", "fsdp"), None),
        P("dp", "fsdp"),
        P(("dp", "fsdp")),
        P("dp"),
    )
    out_specs = P("dp", "fsdp")
    return jax.shard_map(body, mesh=mesh, in_specs=in_specs, out_specs=out_specs, check_vma=False)
```

```python
import functools

import jax
import jax.numpy as jnp
from jax import lax
from jax.experimental import pallas as pl
from jax.experimental.pallas import tpu as pltpu
from jax.sharding import PartitionSpec as P

AXIS = "fsdp"
GROUP = 8
PAIRS = 4
SLOTS = 144
RANK = 64
UNITS = 448
KEYS = GROUP * SLOTS
TOKENS = 768
OWN_TOKENS = 24
FEATURES = 4096
WINDOW = 384
FRONT = 256
HALF = TOKENS // 2
LANES = 2 * (UNITS - FRONT)
TAIL = 16
VMEM_LIMIT = 48 * 1024 * 1024

NEAR = [[GROUP * p + i for i in range(GROUP)] for p in range(PAIRS)]
FAR = [[GROUP * p + i for p in range(PAIRS)] for i in range(GROUP)]


def whole(memory_space=pltpu.VMEM):
    return pl.BlockSpec(memory_space=memory_space)


def params():
    return pltpu.CompilerParams(vmem_limit_bytes=VMEM_LIMIT)


def window_kernel(place_ref, counts_ref, tokens_ref, out_ref, padded, lined):
    padded[:, FEATURES:] = jnp.zeros((OWN_TOKENS, WINDOW), jnp.float32)
    padded[:, :FEATURES] = tokens_ref[...].astype(jnp.float32)
    starts = [jnp.int32(0)]
    for f in range(GROUP * PAIRS - 1):
        starts.append(starts[-1] + counts_ref[f])
    pair = place_ref[0] // GROUP
    lane = lax.broadcasted_iota(jnp.int32, (OWN_TOKENS, WINDOW), 1)
    for target in range(PAIRS):
        for i in range(GROUP):
            start = starts[GROUP * target + i]
            base = pl.multiple_of((start // 128) * 128, 128)
            place = SLOTS * i
            low = (place // 128) * 128
            rest = place - low
            shift = lax.rem(rest - (start - base) + WINDOW, WINDOW)
            moved = pltpu.roll(padded[:, pl.ds(base, WINDOW)], shift, 1)
            keep = (lane >= rest) & (lane < rest + SLOTS)
            lined[:, low : low + WINDOW] = jnp.where(keep, moved, lined[:, low : low + WINDOW])
        out_ref[lax.rem(target - pair + PAIRS, PAIRS)] = lined[:, :KEYS].astype(jnp.bfloat16)


def own_windows(place, counts, tokens):
    return pl.pallas_call(
        window_kernel,
        out_shape=jax.ShapeDtypeStruct((PAIRS, OWN_TOKENS, KEYS), jnp.bfloat16),
        in_specs=[whole(pltpu.SMEM), whole(pltpu.SMEM), whole()],
        out_specs=whole(),
        scratch_shapes=[
            pltpu.VMEM((OWN_TOKENS, FEATURES + WINDOW), jnp.float32),
            pltpu.VMEM((OWN_TOKENS, KEYS + 128), jnp.float32),
        ],
        compiler_params=params(),
    )(place, counts, tokens)


def collect_kernel(place_ref, own_ref, one_ref, two_ref, three_ref, down_ref, out_ref, rows):
    pair = place_ref[0] // GROUP
    blocks = (own_ref[0], one_ref[...], two_ref[...], three_ref[...])
    for step, block in enumerate(blocks):
        origin = lax.rem(pair - step + PAIRS, PAIRS)
        rows[pl.ds(pl.multiple_of(origin * OWN_TOKENS, 8), OWN_TOKENS), :] = block.astype(jnp.float32)
    down = down_ref[...].astype(jnp.float32)
    rows[PAIRS * OWN_TOKENS :, :] = jnp.concatenate(
        [down[8 * g : 8 * g + 8, :] for g in range(SLOTS // 8)], axis=1
    )
    out_ref[...] = rows[...].astype(jnp.bfloat16)


def collect(place, own, one, two, three, down):
    height = PAIRS * OWN_TOKENS + 8
    return pl.pallas_call(
        collect_kernel,
        out_shape=jax.ShapeDtypeStruct((height, KEYS), jnp.bfloat16),
        in_specs=[whole(pltpu.SMEM)] + [whole()] * 5,
        out_specs=whole(),
        scratch_shapes=[pltpu.VMEM((height, KEYS), jnp.float32)],
        compiler_params=params(),
    )(place, own, one, two, three, down)


def offset_of(k, pair):
    last = pair == PAIRS - 1
    return jnp.where(k == 0, jnp.where(last, 1, 3), jnp.where(k == 1, 2, jnp.where(k == 2, jnp.where(last, 3, 1), 0)))


def pack_kernel(place_ref, rows_ref, *out_refs):
    step = pl.program_id(0)
    for k in range(PAIRS):

        @pl.when(step == k)
        def _():
            at = UNITS * (k % 2)
            for i in range(GROUP):
                out_refs[k // 2][i, :, at : at + UNITS] = rows_ref[:, UNITS * i : UNITS * (i + 1)]


def pack(place, rows):
    def block(k, place_ref):
        pair = place_ref[0] // GROUP
        return 0, lax.rem(pair + offset_of(k, pair), PAIRS)

    return pl.pallas_call(
        pack_kernel,
        grid_spec=pltpu.PrefetchScalarGridSpec(
            num_scalar_prefetch=1,
            grid=(PAIRS,),
            in_specs=[pl.BlockSpec((SLOTS, GROUP * UNITS), block)],
            out_specs=[pl.BlockSpec((GROUP, SLOTS, 2 * UNITS), lambda k, _: (0, 0, 0))] * 2,
        ),
        out_shape=[jax.ShapeDtypeStruct((GROUP, SLOTS, 2 * UNITS), jnp.bfloat16)] * 2,
        compiler_params=params(),
    )(place, rows)


def assemble_kernel(place_ref, *refs):
    block_refs, up_refs = refs[:8], refs[8:12]
    tokens_ref, down_ref, up_ref = refs[12:]
    place = place_ref[0]
    pair, side, x = place // GROUP, (place // 4) % 2, place % 4
    for far in range(2):
        for step in range(4):
            block_ref = block_refs[4 * far + step]
            origin = 4 * lax.rem(side + far, 2) + lax.rem(x - step + 4, 4)
            tokens_ref[pl.ds(pl.multiple_of(origin * 96, 96), 96), :] = block_ref[0:96, :]
            folded = block_ref[96:104, :].astype(jnp.float32)
            down_ref[origin] = jnp.concatenate(
                [folded[:, RANK * g : RANK * g + RANK] for g in range(SLOTS // 8)], axis=0
            ).astype(jnp.bfloat16)
    for step, ref in enumerate(up_refs):
        up_ref[lax.rem(pair - step + PAIRS, PAIRS)] = ref[...]


def assemble(place, blocks, ups):
    return pl.pallas_call(
        assemble_kernel,
        out_shape=[
            jax.ShapeDtypeStruct((TOKENS, KEYS), jnp.bfloat16),
            jax.ShapeDtypeStruct((GROUP, SLOTS, RANK), jnp.bfloat16),
            jax.ShapeDtypeStruct((PAIRS, RANK, UNITS), jnp.bfloat16),
        ],
        in_specs=[whole(pltpu.SMEM)] + [whole()] * 12,
        out_specs=[whole()] * 3,
        compiler_params=params(),
    )(place, *blocks, *ups)


def split(total):
    pieces = [total[:, : UNITS // 2], total[:, UNITS // 2 :]]
    rows = []
    for piece in pieces:
        high = piece.astype(jnp.bfloat16).astype(jnp.float32)
        rows += [high, piece - high]
    rows.append(jnp.zeros((TAIL - 4, UNITS // 2), jnp.float32))
    rows = jnp.concatenate(rows, axis=0)
    return jnp.concatenate([rows, jnp.zeros((TAIL, LANES - UNITS // 2), jnp.float32)], axis=1).astype(jnp.bfloat16)


def joined(tail):
    rows = tail.astype(jnp.float32)[:, : UNITS // 2]
    return jnp.concatenate([rows[0:1] + rows[1:2], rows[2:3] + rows[3:4]], axis=1)


def pieces(product):
    back = product[:, FRONT:]
    return product[:, :FRONT], jnp.concatenate([back[:HALF], back[HALF:]], axis=1)


def partial_kernel(stage, place_ref, counts_ref, rows_ref, tokens_ref, down_ref, up_ref, *refs):
    squares_ref, front_ref, back_ref, merged = refs[0], refs[1], refs[2], refs[-1]
    pair = place_ref[0] // GROUP
    row = lax.broadcasted_iota(jnp.int32, (SLOTS, UNITS), 0)
    for k in range(2):
        up = up_ref[lax.rem(pair + offset_of(2 * stage + k, pair), PAIRS)]
        total = jnp.zeros((1, UNITS), jnp.float32)
        for i in range(GROUP):
            low = jnp.dot(down_ref[i], up, preferred_element_type=jnp.float32)
            base = rows_ref[i, :, UNITS * k : UNITS * (k + 1)].astype(jnp.float32)
            value = jnp.where(row < counts_ref[GROUP * pair + i], base + low, 0.0)
            total = total + jnp.sum(value * value, axis=0, keepdims=True)
            merged[SLOTS * i : SLOTS * i + SLOTS, :] = value.astype(jnp.bfloat16)
        product = jnp.dot(tokens_ref[...], merged[...], preferred_element_type=jnp.float32)
        squares_ref[k] = total
        front, back = pieces(product)
        front_ref[k] = front
        back_ref[k] = back
        if stage == 0 and k == 0:
            refs[3][...] = front.astype(jnp.bfloat16)
            refs[4][:HALF] = back.astype(jnp.bfloat16)
            refs[4][HALF:] = split(total)


def partial_products(stage, place, counts, rows, tokens, down, up):
    out_shape = [
        jax.ShapeDtypeStruct((2, 1, UNITS), jnp.float32),
        jax.ShapeDtypeStruct((2, TOKENS, FRONT), jnp.float32),
        jax.ShapeDtypeStruct((2, HALF, LANES), jnp.float32),
    ]
    if stage == 0:
        out_shape += [
            jax.ShapeDtypeStruct((TOKENS, FRONT), jnp.bfloat16),
            jax.ShapeDtypeStruct((HALF + TAIL, LANES), jnp.bfloat16),
        ]
    return pl.pallas_call(
        functools.partial(partial_kernel, stage),
        out_shape=out_shape,
        in_specs=[whole(pltpu.SMEM), whole(pltpu.SMEM)] + [whole()] * 4,
        out_specs=[whole()] * len(out_shape),
        scratch_shapes=[pltpu.VMEM((KEYS, UNITS), jnp.bfloat16)],
        compiler_params=params(),
    )(place, counts, rows, tokens, down, up)


def forward_kernel(step, place_ref, up_got_ref, down_got_ref, early_ref, late_ref, early_squares_ref, late_squares_ref, up_ref, down_ref):
    height = early_ref.shape[1]

    def send(got, own, squares, out):
        out[:height] = (got[:height].astype(jnp.float32) + own).astype(jnp.bfloat16)
        if out.shape[0] > height:
            out[height:] = split(joined(got[height:]) + squares)

    if step == 2:
        send(up_got_ref, early_ref[0], early_squares_ref[0], up_ref)
        send(down_got_ref, early_ref[0], early_squares_ref[0], down_ref)
    else:
        last = place_ref[0] // GROUP == PAIRS - 1
        send(up_got_ref, late_ref[0], late_squares_ref[0], up_ref)
        send(
            down_got_ref,
            jnp.where(last, late_ref[0], early_ref[0]),
            jnp.where(last, late_squares_ref[0], early_squares_ref[0]),
            down_ref,
        )


def forward(step, place, got, early, late, early_squares, late_squares):
    def own(array):
        return pl.BlockSpec((1,) + array.shape[1:], lambda _: (1 if step == 2 else 0, 0, 0))

    moved = pl.BlockSpec(got[0].shape, lambda _: (0, 0))
    return pl.pallas_call(
        functools.partial(forward_kernel, step),
        grid=(1,),
        out_shape=[jax.ShapeDtypeStruct(got[0].shape, jnp.bfloat16)] * 2,
        in_specs=[whole(pltpu.SMEM), moved, moved, own(early), own(late), own(early_squares), own(late_squares)],
        out_specs=[moved, moved],
        compiler_params=params(),
    )(place, *got, early, late, early_squares, late_squares)


def finish_kernel(squares_ref, scale_ref, *refs):
    out_ref = refs[-1]
    own, above, below = refs[0:3]
    front = own[0] + above[...].astype(jnp.float32) + below[...].astype(jnp.float32)
    own, above, below = refs[3:6]
    back = own[0] + above[:HALF].astype(jnp.float32) + below[:HALF].astype(jnp.float32)
    width = back.shape[1] // 2
    back = jnp.concatenate([back[:, :width], back[:, width:]], axis=0)
    total = squares_ref[0] + joined(above[HALF:]) + joined(below[HALF:])
    factor = scale_ref[...].astype(jnp.float32) / jnp.sqrt(total + 1e-06)
    result = jnp.concatenate([front, back], axis=1)
    result = jnp.where(factor == 0.0, 0.0, result * factor)
    out_ref[...] = jnp.concatenate(
        [
            result[OWN_TOKENS * (PAIRS * i + q) : OWN_TOKENS * (PAIRS * i + q + 1), :]
            for q in range(PAIRS)
            for i in range(GROUP)
        ],
        axis=0,
    ).astype(jnp.bfloat16)


def finish(squares, scale, front, back, sums):
    def at(index, *shape):
        return pl.BlockSpec(shape, lambda _: (index,) + (0,) * (len(shape) - 1))

    def same(array):
        return pl.BlockSpec(array.shape, lambda _: (0, 0))

    return pl.pallas_call(
        finish_kernel,
        grid=(1,),
        out_shape=jax.ShapeDtypeStruct((TOKENS, UNITS), jnp.bfloat16),
        in_specs=[at(1, 1, 1, UNITS), same(scale)]
        + [at(1, 1, TOKENS, FRONT), same(sums[0]), same(sums[1])]
        + [at(1, 1, HALF, LANES), same(sums[2]), same(sums[3])],
        out_specs=pl.BlockSpec((TOKENS, UNITS), lambda _: (0, 0)),
        compiler_params=params(),
    )(squares, scale, front, sums[0], sums[1], back, sums[2], sums[3])


def to_pair(array, step):
    return lax.ppermute(
        array,
        AXIS,
        [(GROUP * p + i, GROUP * ((p + step) % PAIRS) + i) for p in range(PAIRS) for i in range(GROUP)],
    )


def along_x(array, step):
    return lax.ppermute(array, AXIS, [(4 * z + x, 4 * z + (x + step) % 4) for z in range(8) for x in range(4)])


def hop(array, froms, way):
    return lax.ppermute(
        array, AXIS, [(GROUP * p + i, GROUP * (p + way) + i) for p in froms for i in range(GROUP)]
    )


def hops(sends, step):
    return hop(sends[0], range(step), 1), hop(sends[1], range(PAIRS - step, PAIRS), -1)


def exchange(send):
    return lax.all_to_all(send, AXIS, 0, 0, axis_index_groups=NEAR, tiled=True)


def body(tokens, frozen_slot_rows, adapter_down_factor, adapter_up_factor, magnitude, counts):
    place = lax.axis_index(AXIS).astype(jnp.int32).reshape(1)
    own = own_windows(place, counts, tokens)
    moved = [to_pair(own[step], step) for step in range(1, PAIRS)]
    ups = [adapter_up_factor] + [to_pair(adapter_up_factor, step) for step in range(1, PAIRS)]
    frozen_slot_rows, moved[0] = lax.optimization_barrier((frozen_slot_rows, moved[0]))
    sends = list(pack(place, frozen_slot_rows))
    column = collect(place, own, *moved, adapter_down_factor)
    other = lax.ppermute(column, AXIS, [(f, f ^ 4) for f in range(GROUP * PAIRS)])
    blocks = [column] + [along_x(column, step) for step in range(1, 4)]
    blocks += [other] + [along_x(other, step) for step in range(1, 4)]
    sends[0], blocks[5] = lax.optimization_barrier((sends[0], blocks[5]))
    rows = exchange(sends[0])
    all_tokens, down, up = assemble(place, blocks, ups)
    early_squares, early_front, early_back, first_front, first_back = partial_products(
        0, place, counts, rows, all_tokens, down, up
    )
    sends[1], early_front = lax.optimization_barrier((sends[1], early_front))
    a, b = hops((first_front, first_front), 1), hops((first_back, first_back), 1)
    rows = exchange(sends[1])
    a = hops(forward(2, place, a, early_front, early_front, early_squares, early_squares), 2)
    b = hops(forward(2, place, b, early_back, early_back, early_squares, early_squares), 2)
    rows, *a = lax.optimization_barrier((rows, *a))
    squares, front, back = partial_products(1, place, counts, rows, all_tokens, down, up)
    a = hops(forward(3, place, a, early_front, front, early_squares, squares), 3)
    b = hops(forward(3, place, b, early_back, back, early_squares, squares), 3)
    return finish(squares, magnitude.reshape(1, UNITS), front, back, [*a, *b])


def solution(mesh):
    in_specs = (
        P(("dp", "fsdp"), None),
        P(("dp", "fsdp"), None),
        P(("dp", "fsdp"), None),
        P("dp", "fsdp"),
        P(("dp", "fsdp")),
        P("dp"),
    )
    out_specs = P("dp", "fsdp")
    return jax.shard_map(body, mesh=mesh, in_specs=in_specs, out_specs=out_specs, check_vma=False)
```

```python
import functools

import jax
import jax.numpy as jnp
from jax import lax
from jax.experimental import pallas as pl
from jax.experimental.pallas import tpu as pltpu
from jax.sharding import PartitionSpec as P

AXIS = "fsdp"
GROUP = 8
PAIRS = 4
SLOTS = 144
RANK = 64
UNITS = 448
KEYS = GROUP * SLOTS
TOKENS = 768
OWN_TOKENS = 24
FEATURES = 4096
WINDOW = 384
PARTS = ((0, 1), (2, 3))
FRONT = 256
HALF = TOKENS // 2
LANES = 2 * (UNITS - FRONT)
TAIL = 16
VMEM_LIMIT = 48 * 1024 * 1024

NEAR = [[GROUP * p + i for i in range(GROUP)] for p in range(PAIRS)]
FAR = [[GROUP * p + i for p in range(PAIRS)] for i in range(GROUP)]


def whole(memory_space=pltpu.VMEM):
    return pl.BlockSpec(memory_space=memory_space)


def params():
    return pltpu.CompilerParams(vmem_limit_bytes=VMEM_LIMIT)


def window_kernel(place_ref, counts_ref, tokens_ref, out_ref, padded, lined):
    padded[:, FEATURES:] = jnp.zeros((OWN_TOKENS, WINDOW), jnp.float32)
    padded[:, :FEATURES] = tokens_ref[...].astype(jnp.float32)
    starts = [jnp.int32(0)]
    for f in range(GROUP * PAIRS - 1):
        starts.append(starts[-1] + counts_ref[f])
    pair = place_ref[0] // GROUP
    lane = lax.broadcasted_iota(jnp.int32, (OWN_TOKENS, WINDOW), 1)
    for target in range(PAIRS):
        for i in range(GROUP):
            start = starts[GROUP * target + i]
            base = pl.multiple_of((start // 128) * 128, 128)
            place = SLOTS * i
            low = (place // 128) * 128
            rest = place - low
            shift = lax.rem(rest - (start - base) + WINDOW, WINDOW)
            moved = pltpu.roll(padded[:, pl.ds(base, WINDOW)], shift, 1)
            keep = (lane >= rest) & (lane < rest + SLOTS)
            lined[:, low : low + WINDOW] = jnp.where(keep, moved, lined[:, low : low + WINDOW])
        out_ref[lax.rem(target - pair + PAIRS, PAIRS)] = lined[:, :KEYS].astype(jnp.bfloat16)


def own_windows(place, counts, tokens):
    return pl.pallas_call(
        window_kernel,
        out_shape=jax.ShapeDtypeStruct((PAIRS, OWN_TOKENS, KEYS), jnp.bfloat16),
        in_specs=[whole(pltpu.SMEM), whole(pltpu.SMEM), whole()],
        out_specs=whole(),
        scratch_shapes=[
            pltpu.VMEM((OWN_TOKENS, FEATURES + WINDOW), jnp.float32),
            pltpu.VMEM((OWN_TOKENS, KEYS + 128), jnp.float32),
        ],
        compiler_params=params(),
    )(place, counts, tokens)


def collect_kernel(place_ref, own_ref, one_ref, two_ref, three_ref, down_ref, out_ref, rows):
    pair = place_ref[0] // GROUP
    blocks = (own_ref[0], one_ref[...], two_ref[...], three_ref[...])
    for step, block in enumerate(blocks):
        origin = lax.rem(pair - step + PAIRS, PAIRS)
        rows[pl.ds(pl.multiple_of(origin * OWN_TOKENS, 8), OWN_TOKENS), :] = block.astype(jnp.float32)
    down = down_ref[...].astype(jnp.float32)
    rows[PAIRS * OWN_TOKENS :, :] = jnp.concatenate(
        [down[8 * g : 8 * g + 8, :] for g in range(SLOTS // 8)], axis=1
    )
    out_ref[...] = rows[...].astype(jnp.bfloat16)


def collect(place, own, one, two, three, down):
    height = PAIRS * OWN_TOKENS + 8
    return pl.pallas_call(
        collect_kernel,
        out_shape=jax.ShapeDtypeStruct((height, KEYS), jnp.bfloat16),
        in_specs=[whole(pltpu.SMEM)] + [whole()] * 5,
        out_specs=whole(),
        scratch_shapes=[pltpu.VMEM((height, KEYS), jnp.float32)],
        compiler_params=params(),
    )(place, own, one, two, three, down)


def offset_of(k, pair):
    last = pair == PAIRS - 1
    return jnp.where(k == 0, jnp.where(last, 1, 3), jnp.where(k == 1, 2, jnp.where(k == 2, jnp.where(last, 3, 1), 0)))


def pack_kernel(ks, place_ref, rows_ref, *out_refs):
    step = pl.program_id(0)
    for n, (part, at) in enumerate(ks):

        @pl.when(step == n)
        def _():
            for i in range(GROUP):
                out_refs[part][i, :, UNITS * at : UNITS * (at + 1)] = rows_ref[:, UNITS * i : UNITS * (i + 1)]


def pack(place, rows, parts):
    ks = [(n, at) for n, part in enumerate(parts) for at in range(len(part))]
    first = parts[0][0]

    def block(n, place_ref):
        pair = place_ref[0] // GROUP
        return 0, lax.rem(pair + offset_of(n + first, pair), PAIRS)

    return list(pl.pallas_call(
        functools.partial(pack_kernel, ks),
        grid_spec=pltpu.PrefetchScalarGridSpec(
            num_scalar_prefetch=1,
            grid=(len(ks),),
            in_specs=[pl.BlockSpec((SLOTS, GROUP * UNITS), block)],
            out_specs=[pl.BlockSpec((GROUP, SLOTS, len(part) * UNITS), lambda n, _: (0, 0, 0)) for part in parts],
        ),
        out_shape=[jax.ShapeDtypeStruct((GROUP, SLOTS, len(part) * UNITS), jnp.bfloat16) for part in parts],
        compiler_params=params(),
    )(place, rows))


def assemble_kernel(place_ref, *refs):
    block_refs, up_refs = refs[:4], refs[4:8]
    tokens_ref, down_ref, up_ref = refs[8:]
    place = place_ref[0]
    pair, side, x = place // GROUP, (place // 4) % 2, place % 4
    for step, block_ref in enumerate(block_refs):
        for far in range(2):
            origin = 4 * lax.rem(side + far, 2) + lax.rem(x - step + 4, 4)
            tokens_ref[pl.ds(pl.multiple_of(origin * 96, 96), 96), :] = block_ref[far, 0:96, :]
            folded = block_ref[far, 96:104, :].astype(jnp.float32)
            down_ref[origin] = jnp.concatenate(
                [folded[:, RANK * g : RANK * g + RANK] for g in range(SLOTS // 8)], axis=0
            ).astype(jnp.bfloat16)
    for step, ref in enumerate(up_refs):
        up_ref[lax.rem(pair - step + PAIRS, PAIRS)] = ref[...]


def assemble(place, blocks, ups):
    return pl.pallas_call(
        assemble_kernel,
        out_shape=[
            jax.ShapeDtypeStruct((TOKENS, KEYS), jnp.bfloat16),
            jax.ShapeDtypeStruct((GROUP, SLOTS, RANK), jnp.bfloat16),
            jax.ShapeDtypeStruct((PAIRS, RANK, UNITS), jnp.bfloat16),
        ],
        in_specs=[whole(pltpu.SMEM)] + [whole()] * 8,
        out_specs=[whole()] * 3,
        compiler_params=params(),
    )(place, *blocks, *ups)


def split(total):
    pieces = [total[:, : UNITS // 2], total[:, UNITS // 2 :]]
    rows = []
    for piece in pieces:
        high = piece.astype(jnp.bfloat16).astype(jnp.float32)
        rows += [high, piece - high]
    rows.append(jnp.zeros((TAIL - 4, UNITS // 2), jnp.float32))
    rows = jnp.concatenate(rows, axis=0)
    return jnp.concatenate([rows, jnp.zeros((TAIL, LANES - UNITS // 2), jnp.float32)], axis=1).astype(jnp.bfloat16)


def joined(tail):
    rows = tail.astype(jnp.float32)[:, : UNITS // 2]
    return jnp.concatenate([rows[0:1] + rows[1:2], rows[2:3] + rows[3:4]], axis=1)


def pieces(product):
    back = product[:, FRONT:]
    return product[:, :FRONT], jnp.concatenate([back[:HALF], back[HALF:]], axis=1)


def partial_kernel(stage, place_ref, counts_ref, rows_ref, tokens_ref, down_ref, up_ref, *refs):
    squares_ref, front_ref, back_ref, merged = refs[0], refs[1], refs[2], refs[-1]
    pair = place_ref[0] // GROUP
    row = lax.broadcasted_iota(jnp.int32, (SLOTS, UNITS), 0)
    for k in range(2):
        up = up_ref[lax.rem(pair + offset_of(2 * stage + k, pair), PAIRS)]
        total = jnp.zeros((1, UNITS), jnp.float32)
        for i in range(GROUP):
            low = jnp.dot(down_ref[i], up, preferred_element_type=jnp.float32)
            base = rows_ref[i, :, UNITS * k : UNITS * (k + 1)].astype(jnp.float32)
            value = jnp.where(row < counts_ref[GROUP * pair + i], base + low, 0.0)
            total = total + jnp.sum(value * value, axis=0, keepdims=True)
            merged[SLOTS * i : SLOTS * i + SLOTS, :] = value.astype(jnp.bfloat16)
        product = jnp.dot(tokens_ref[...], merged[...], preferred_element_type=jnp.float32)
        squares_ref[k] = total
        front, back = pieces(product)
        front_ref[k] = front
        back_ref[k] = back
        if stage == 0 and k == 0:
            refs[3][...] = front.astype(jnp.bfloat16)
            refs[4][:HALF] = back.astype(jnp.bfloat16)
            refs[4][HALF:] = split(total)


def partial_products(stage, place, counts, rows, tokens, down, up):
    out_shape = [
        jax.ShapeDtypeStruct((2, 1, UNITS), jnp.float32),
        jax.ShapeDtypeStruct((2, TOKENS, FRONT), jnp.float32),
        jax.ShapeDtypeStruct((2, HALF, LANES), jnp.float32),
    ]
    if stage == 0:
        out_shape += [
            jax.ShapeDtypeStruct((TOKENS, FRONT), jnp.bfloat16),
            jax.ShapeDtypeStruct((HALF + TAIL, LANES), jnp.bfloat16),
        ]
    return pl.pallas_call(
        functools.partial(partial_kernel, stage),
        out_shape=out_shape,
        in_specs=[whole(pltpu.SMEM), whole(pltpu.SMEM)] + [whole()] * 4,
        out_specs=[whole()] * len(out_shape),
        scratch_shapes=[pltpu.VMEM((KEYS, UNITS), jnp.bfloat16)],
        compiler_params=params(),
    )(place, counts, rows, tokens, down, up)


def forward_kernel(step, place_ref, up_got_ref, down_got_ref, early_ref, late_ref, early_squares_ref, late_squares_ref, up_ref, down_ref):
    height = early_ref.shape[1]

    def send(got, own, squares, out):
        out[:height] = (got[:height].astype(jnp.float32) + own).astype(jnp.bfloat16)
        if out.shape[0] > height:
            out[height:] = split(joined(got[height:]) + squares)

    if step == 2:
        send(up_got_ref, early_ref[0], early_squares_ref[0], up_ref)
        send(down_got_ref, early_ref[0], early_squares_ref[0], down_ref)
    else:
        last = place_ref[0] // GROUP == PAIRS - 1
        send(up_got_ref, late_ref[0], late_squares_ref[0], up_ref)
        send(
            down_got_ref,
            jnp.where(last, late_ref[0], early_ref[0]),
            jnp.where(last, late_squares_ref[0], early_squares_ref[0]),
            down_ref,
        )


def forward(step, place, got, early, late, early_squares, late_squares):
    def own(array):
        return pl.BlockSpec((1,) + array.shape[1:], lambda _: (1 if step == 2 else 0, 0, 0))

    moved = pl.BlockSpec(got[0].shape, lambda _: (0, 0))
    return pl.pallas_call(
        functools.partial(forward_kernel, step),
        grid=(1,),
        out_shape=[jax.ShapeDtypeStruct(got[0].shape, jnp.bfloat16)] * 2,
        in_specs=[whole(pltpu.SMEM), moved, moved, own(early), own(late), own(early_squares), own(late_squares)],
        out_specs=[moved, moved],
        compiler_params=params(),
    )(place, *got, early, late, early_squares, late_squares)


def finish_kernel(squares_ref, scale_ref, *refs):
    out_ref = refs[-1]
    own, above, below = refs[0:3]
    front = own[0] + above[...].astype(jnp.float32) + below[...].astype(jnp.float32)
    own, above, below = refs[3:6]
    back = own[0] + above[:HALF].astype(jnp.float32) + below[:HALF].astype(jnp.float32)
    width = back.shape[1] // 2
    back = jnp.concatenate([back[:, :width], back[:, width:]], axis=0)
    total = squares_ref[0] + joined(above[HALF:]) + joined(below[HALF:])
    factor = scale_ref[...].astype(jnp.float32) / jnp.sqrt(total + 1e-06)
    result = jnp.concatenate([front, back], axis=1)
    result = jnp.where(factor == 0.0, 0.0, result * factor)
    out_ref[...] = jnp.concatenate(
        [
            result[OWN_TOKENS * (PAIRS * i + q) : OWN_TOKENS * (PAIRS * i + q + 1), :]
            for q in range(PAIRS)
            for i in range(GROUP)
        ],
        axis=0,
    ).astype(jnp.bfloat16)


def finish(squares, scale, front, back, sums):
    def at(index, *shape):
        return pl.BlockSpec(shape, lambda _: (index,) + (0,) * (len(shape) - 1))

    def same(array):
        return pl.BlockSpec(array.shape, lambda _: (0, 0))

    return pl.pallas_call(
        finish_kernel,
        grid=(1,),
        out_shape=jax.ShapeDtypeStruct((TOKENS, UNITS), jnp.bfloat16),
        in_specs=[at(1, 1, 1, UNITS), same(scale)]
        + [at(1, 1, TOKENS, FRONT), same(sums[0]), same(sums[1])]
        + [at(1, 1, HALF, LANES), same(sums[2]), same(sums[3])],
        out_specs=pl.BlockSpec((TOKENS, UNITS), lambda _: (0, 0)),
        compiler_params=params(),
    )(squares, scale, front, sums[0], sums[1], back, sums[2], sums[3])


def to_pair(array, step):
    return lax.ppermute(
        array,
        AXIS,
        [(GROUP * p + i, GROUP * ((p + step) % PAIRS) + i) for p in range(PAIRS) for i in range(GROUP)],
    )


def along_x(array, step):
    return lax.ppermute(array, AXIS, [(4 * z + x, 4 * z + (x + step) % 4) for z in range(8) for x in range(4)])


def hop(array, froms, way):
    return lax.ppermute(
        array, AXIS, [(GROUP * p + i, GROUP * (p + way) + i) for p in froms for i in range(GROUP)]
    )


def hops(sends, step):
    return hop(sends[0], range(step), 1), hop(sends[1], range(PAIRS - step, PAIRS), -1)


def exchange(send):
    return lax.all_to_all(send, AXIS, 0, 0, axis_index_groups=NEAR, tiled=True)


def body(tokens, frozen_slot_rows, adapter_down_factor, adapter_up_factor, magnitude, counts):
    place = lax.axis_index(AXIS).astype(jnp.int32).reshape(1)
    own = own_windows(place, counts, tokens)
    moved = [to_pair(own[step], step) for step in range(1, PAIRS)]
    ups = [adapter_up_factor] + [to_pair(adapter_up_factor, step) for step in range(1, PAIRS)]
    column = collect(place, own, *moved, adapter_down_factor)
    other = lax.ppermute(column, AXIS, [(f, f ^ 4) for f in range(GROUP * PAIRS)])
    frozen_slot_rows, column = lax.optimization_barrier((frozen_slot_rows, column))
    sends = pack(place, frozen_slot_rows, PARTS[:1])
    sends[0], other = lax.optimization_barrier((sends[0], other))
    rows = exchange(sends[0])
    frozen_slot_rows, other = lax.optimization_barrier((frozen_slot_rows, other))
    sends += pack(place, frozen_slot_rows, PARTS[1:])
    blocks = jnp.stack([column, other])
    blocks = [blocks] + [along_x(blocks, step) for step in range(1, 4)]
    all_tokens, down, up = assemble(place, blocks, ups)
    early_squares, early_front, early_back, first_front, first_back = partial_products(
        0, place, counts, rows, all_tokens, down, up
    )
    sends[1], early_front = lax.optimization_barrier((sends[1], early_front))
    a, b = hops((first_front, first_front), 1), hops((first_back, first_back), 1)
    rows = exchange(sends[1])
    a = hops(forward(2, place, a, early_front, early_front, early_squares, early_squares), 2)
    b = hops(forward(2, place, b, early_back, early_back, early_squares, early_squares), 2)
    rows, *a = lax.optimization_barrier((rows, *a))
    squares, front, back = partial_products(1, place, counts, rows, all_tokens, down, up)
    a = hops(forward(3, place, a, early_front, front, early_squares, squares), 3)
    b = hops(forward(3, place, b, early_back, back, early_squares, squares), 3)
    return finish(squares, magnitude.reshape(1, UNITS), front, back, [*a, *b])


def solution(mesh):
    in_specs = (
        P(("dp", "fsdp"), None),
        P(("dp", "fsdp"), None),
        P(("dp", "fsdp"), None),
        P("dp", "fsdp"),
        P(("dp", "fsdp")),
        P("dp"),
    )
    out_specs = P("dp", "fsdp")
    return jax.shard_map(body, mesh=mesh, in_specs=in_specs, out_specs=out_specs, check_vma=False)
```

```python
import functools

import jax
import jax.numpy as jnp
from jax import lax
from jax.experimental import pallas as pl
from jax.experimental.pallas import tpu as pltpu
from jax.sharding import PartitionSpec as P

AXIS = "fsdp"
GROUP = 8
PAIRS = 4
SLOTS = 144
RANK = 64
UNITS = 448
KEYS = GROUP * SLOTS
TOKENS = 768
OWN_TOKENS = 24
FEATURES = 4096
WINDOW = 384
PARTS = ((0, 1), (2, 3))
FRONT = 256
HALF = TOKENS // 2
LANES = 2 * (UNITS - FRONT)
TAIL = 16
VMEM_LIMIT = 48 * 1024 * 1024

NEAR = [[GROUP * p + i for i in range(GROUP)] for p in range(PAIRS)]
FAR = [[GROUP * p + i for p in range(PAIRS)] for i in range(GROUP)]


def whole(memory_space=pltpu.VMEM):
    return pl.BlockSpec(memory_space=memory_space)


def params():
    return pltpu.CompilerParams(vmem_limit_bytes=VMEM_LIMIT)


def window_kernel(place_ref, counts_ref, tokens_ref, out_ref, padded, lined):
    padded[:, FEATURES:] = jnp.zeros((OWN_TOKENS, WINDOW), jnp.float32)
    padded[:, :FEATURES] = tokens_ref[...].astype(jnp.float32)
    starts = [jnp.int32(0)]
    for f in range(GROUP * PAIRS - 1):
        starts.append(starts[-1] + counts_ref[f])
    pair = place_ref[0] // GROUP
    lane = lax.broadcasted_iota(jnp.int32, (OWN_TOKENS, WINDOW), 1)
    for target in range(PAIRS):
        for i in range(GROUP):
            start = starts[GROUP * target + i]
            base = pl.multiple_of((start // 128) * 128, 128)
            place = SLOTS * i
            low = (place // 128) * 128
            rest = place - low
            shift = lax.rem(rest - (start - base) + WINDOW, WINDOW)
            moved = pltpu.roll(padded[:, pl.ds(base, WINDOW)], shift, 1)
            keep = (lane >= rest) & (lane < rest + SLOTS)
            lined[:, low : low + WINDOW] = jnp.where(keep, moved, lined[:, low : low + WINDOW])
        out_ref[lax.rem(target - pair + PAIRS, PAIRS)] = lined[:, :KEYS].astype(jnp.bfloat16)


def own_windows(place, counts, tokens):
    return pl.pallas_call(
        window_kernel,
        out_shape=jax.ShapeDtypeStruct((PAIRS, OWN_TOKENS, KEYS), jnp.bfloat16),
        in_specs=[whole(pltpu.SMEM), whole(pltpu.SMEM), whole()],
        out_specs=whole(),
        scratch_shapes=[
            pltpu.VMEM((OWN_TOKENS, FEATURES + WINDOW), jnp.float32),
            pltpu.VMEM((OWN_TOKENS, KEYS + 128), jnp.float32),
        ],
        compiler_params=params(),
    )(place, counts, tokens)


def collect_kernel(place_ref, own_ref, one_ref, two_ref, three_ref, down_ref, out_ref, rows):
    pair = place_ref[0] // GROUP
    blocks = (own_ref[0], one_ref[...], two_ref[...], three_ref[...])
    for step, block in enumerate(blocks):
        origin = lax.rem(pair - step + PAIRS, PAIRS)
        rows[pl.ds(pl.multiple_of(origin * OWN_TOKENS, 8), OWN_TOKENS), :] = block.astype(jnp.float32)
    down = down_ref[...].astype(jnp.float32)
    rows[PAIRS * OWN_TOKENS :, :] = jnp.concatenate(
        [down[8 * g : 8 * g + 8, :] for g in range(SLOTS // 8)], axis=1
    )
    out_ref[...] = rows[...].astype(jnp.bfloat16)


def collect(place, own, one, two, three, down):
    height = PAIRS * OWN_TOKENS + 8
    return pl.pallas_call(
        collect_kernel,
        out_shape=jax.ShapeDtypeStruct((height, KEYS), jnp.bfloat16),
        in_specs=[whole(pltpu.SMEM)] + [whole()] * 5,
        out_specs=whole(),
        scratch_shapes=[pltpu.VMEM((height, KEYS), jnp.float32)],
        compiler_params=params(),
    )(place, own, one, two, three, down)


def offset_of(k, pair):
    last = pair == PAIRS - 1
    return jnp.where(k == 0, jnp.where(last, 1, 3), jnp.where(k == 1, 2, jnp.where(k == 2, jnp.where(last, 3, 1), 0)))


def pack_kernel(ks, place_ref, rows_ref, *out_refs):
    step = pl.program_id(0)
    for n, (part, at) in enumerate(ks):

        @pl.when(step == n)
        def _():
            for i in range(GROUP):
                out_refs[part][i, :, UNITS * at : UNITS * (at + 1)] = rows_ref[:, UNITS * i : UNITS * (i + 1)]


def pack(place, rows, parts):
    ks = [(n, at) for n, part in enumerate(parts) for at in range(len(part))]
    first = parts[0][0]

    def block(n, place_ref):
        pair = place_ref[0] // GROUP
        return 0, lax.rem(pair + offset_of(n + first, pair), PAIRS)

    return list(pl.pallas_call(
        functools.partial(pack_kernel, ks),
        grid_spec=pltpu.PrefetchScalarGridSpec(
            num_scalar_prefetch=1,
            grid=(len(ks),),
            in_specs=[pl.BlockSpec((SLOTS, GROUP * UNITS), block)],
            out_specs=[pl.BlockSpec((GROUP, SLOTS, len(part) * UNITS), lambda n, _: (0, 0, 0)) for part in parts],
        ),
        out_shape=[jax.ShapeDtypeStruct((GROUP, SLOTS, len(part) * UNITS), jnp.bfloat16) for part in parts],
        compiler_params=params(),
    )(place, rows))


def assemble_kernel(place_ref, *refs):
    block_refs, up_refs = refs[:4], refs[4:8]
    tokens_ref, down_ref, up_ref = refs[8:]
    place = place_ref[0]
    pair, side, x = place // GROUP, (place // 4) % 2, place % 4
    for step, block_ref in enumerate(block_refs):
        for far in range(2):
            origin = 4 * lax.rem(side + far, 2) + lax.rem(x - step + 4, 4)
            tokens_ref[pl.ds(pl.multiple_of(origin * 96, 96), 96), :] = block_ref[far, 0:96, :]
            folded = block_ref[far, 96:104, :].astype(jnp.float32)
            down_ref[origin] = jnp.concatenate(
                [folded[:, RANK * g : RANK * g + RANK] for g in range(SLOTS // 8)], axis=0
            ).astype(jnp.bfloat16)
    for step, ref in enumerate(up_refs):
        up_ref[lax.rem(pair - step + PAIRS, PAIRS)] = ref[...]


def assemble(place, blocks, ups):
    return pl.pallas_call(
        assemble_kernel,
        out_shape=[
            jax.ShapeDtypeStruct((TOKENS, KEYS), jnp.bfloat16),
            jax.ShapeDtypeStruct((GROUP, SLOTS, RANK), jnp.bfloat16),
            jax.ShapeDtypeStruct((PAIRS, RANK, UNITS), jnp.bfloat16),
        ],
        in_specs=[whole(pltpu.SMEM)] + [whole()] * 8,
        out_specs=[whole()] * 3,
        compiler_params=params(),
    )(place, *blocks, *ups)


def split(total):
    pieces = [total[:, : UNITS // 2], total[:, UNITS // 2 :]]
    rows = []
    for piece in pieces:
        high = piece.astype(jnp.bfloat16).astype(jnp.float32)
        rows += [high, piece - high]
    rows.append(jnp.zeros((TAIL - 4, UNITS // 2), jnp.float32))
    rows = jnp.concatenate(rows, axis=0)
    return jnp.concatenate([rows, jnp.zeros((TAIL, LANES - UNITS // 2), jnp.float32)], axis=1).astype(jnp.bfloat16)


def joined(tail):
    rows = tail.astype(jnp.float32)[:, : UNITS // 2]
    return jnp.concatenate([rows[0:1] + rows[1:2], rows[2:3] + rows[3:4]], axis=1)


def pieces(product):
    back = product[:, FRONT:]
    return product[:, :FRONT], jnp.concatenate([back[:HALF], back[HALF:]], axis=1)


def partial_kernel(stage, place_ref, counts_ref, rows_ref, tokens_ref, down_ref, up_ref, *refs):
    squares_ref, front_ref, back_ref, merged = refs[0], refs[1], refs[2], refs[-1]
    pair = place_ref[0] // GROUP
    row = lax.broadcasted_iota(jnp.int32, (SLOTS, UNITS), 0)
    for k in range(2):
        up = up_ref[lax.rem(pair + offset_of(2 * stage + k, pair), PAIRS)]
        total = jnp.zeros((1, UNITS), jnp.float32)
        for i in range(GROUP):
            low = jnp.dot(down_ref[i], up, preferred_element_type=jnp.float32)
            base = rows_ref[i, :, UNITS * k : UNITS * (k + 1)].astype(jnp.float32)
            value = jnp.where(row < counts_ref[GROUP * pair + i], base + low, 0.0)
            total = total + jnp.sum(value * value, axis=0, keepdims=True)
            merged[SLOTS * i : SLOTS * i + SLOTS, :] = value.astype(jnp.bfloat16)
        product = jnp.dot(tokens_ref[...], merged[...], preferred_element_type=jnp.float32)
        squares_ref[k] = total
        front, back = pieces(product)
        front_ref[k] = front
        back_ref[k] = back
        if stage == 0 and k == 0:
            refs[3][...] = front.astype(jnp.bfloat16)
            refs[4][:HALF] = back.astype(jnp.bfloat16)
            refs[4][HALF:] = split(total)


def partial_products(stage, place, counts, rows, tokens, down, up):
    out_shape = [
        jax.ShapeDtypeStruct((2, 1, UNITS), jnp.float32),
        jax.ShapeDtypeStruct((2, TOKENS, FRONT), jnp.float32),
        jax.ShapeDtypeStruct((2, HALF, LANES), jnp.float32),
    ]
    if stage == 0:
        out_shape += [
            jax.ShapeDtypeStruct((TOKENS, FRONT), jnp.bfloat16),
            jax.ShapeDtypeStruct((HALF + TAIL, LANES), jnp.bfloat16),
        ]
    return pl.pallas_call(
        functools.partial(partial_kernel, stage),
        out_shape=out_shape,
        in_specs=[whole(pltpu.SMEM), whole(pltpu.SMEM)] + [whole()] * 4,
        out_specs=[whole()] * len(out_shape),
        scratch_shapes=[pltpu.VMEM((KEYS, UNITS), jnp.bfloat16)],
        compiler_params=params(),
    )(place, counts, rows, tokens, down, up)


def forward_kernel(step, place_ref, up_got_ref, down_got_ref, early_ref, late_ref, early_squares_ref, late_squares_ref, up_ref, down_ref):
    height = early_ref.shape[1]

    def send(got, own, squares, out):
        out[:height] = (got[:height].astype(jnp.float32) + own).astype(jnp.bfloat16)
        if out.shape[0] > height:
            out[height:] = split(joined(got[height:]) + squares)

    if step == 2:
        send(up_got_ref, early_ref[0], early_squares_ref[0], up_ref)
        send(down_got_ref, early_ref[0], early_squares_ref[0], down_ref)
    else:
        last = place_ref[0] // GROUP == PAIRS - 1
        send(up_got_ref, late_ref[0], late_squares_ref[0], up_ref)
        send(
            down_got_ref,
            jnp.where(last, late_ref[0], early_ref[0]),
            jnp.where(last, late_squares_ref[0], early_squares_ref[0]),
            down_ref,
        )


def forward(step, place, got, early, late, early_squares, late_squares):
    def own(array):
        return pl.BlockSpec((1,) + array.shape[1:], lambda _: (1 if step == 2 else 0, 0, 0))

    moved = pl.BlockSpec(got[0].shape, lambda _: (0, 0))
    return pl.pallas_call(
        functools.partial(forward_kernel, step),
        grid=(1,),
        out_shape=[jax.ShapeDtypeStruct(got[0].shape, jnp.bfloat16)] * 2,
        in_specs=[whole(pltpu.SMEM), moved, moved, own(early), own(late), own(early_squares), own(late_squares)],
        out_specs=[moved, moved],
        compiler_params=params(),
    )(place, *got, early, late, early_squares, late_squares)


def finish_kernel(squares_ref, scale_ref, *refs):
    out_ref = refs[-1]
    own, above, below = refs[0:3]
    front = own[0] + above[...].astype(jnp.float32) + below[...].astype(jnp.float32)
    own, above, below = refs[3:6]
    back = own[0] + above[:HALF].astype(jnp.float32) + below[:HALF].astype(jnp.float32)
    width = back.shape[1] // 2
    back = jnp.concatenate([back[:, :width], back[:, width:]], axis=0)
    total = squares_ref[0] + joined(above[HALF:]) + joined(below[HALF:])
    factor = scale_ref[...].astype(jnp.float32) / jnp.sqrt(total + 1e-06)
    result = jnp.concatenate([front, back], axis=1)
    result = jnp.where(factor == 0.0, 0.0, result * factor)
    out_ref[...] = jnp.concatenate(
        [
            result[OWN_TOKENS * (PAIRS * i + q) : OWN_TOKENS * (PAIRS * i + q + 1), :]
            for q in range(PAIRS)
            for i in range(GROUP)
        ],
        axis=0,
    ).astype(jnp.bfloat16)


def finish(squares, scale, front, back, sums):
    def at(index, *shape):
        return pl.BlockSpec(shape, lambda _: (index,) + (0,) * (len(shape) - 1))

    def same(array):
        return pl.BlockSpec(array.shape, lambda _: (0, 0))

    return pl.pallas_call(
        finish_kernel,
        grid=(1,),
        out_shape=jax.ShapeDtypeStruct((TOKENS, UNITS), jnp.bfloat16),
        in_specs=[at(1, 1, 1, UNITS), same(scale)]
        + [at(1, 1, TOKENS, FRONT), same(sums[0]), same(sums[1])]
        + [at(1, 1, HALF, LANES), same(sums[2]), same(sums[3])],
        out_specs=pl.BlockSpec((TOKENS, UNITS), lambda _: (0, 0)),
        compiler_params=params(),
    )(squares, scale, front, sums[0], sums[1], back, sums[2], sums[3])


def to_pair(array, step):
    return lax.ppermute(
        array,
        AXIS,
        [(GROUP * p + i, GROUP * ((p + step) % PAIRS) + i) for p in range(PAIRS) for i in range(GROUP)],
    )


def along_x(array, step):
    return lax.ppermute(array, AXIS, [(4 * z + x, 4 * z + (x + step) % 4) for z in range(8) for x in range(4)])


def hop(array, froms, way):
    return lax.ppermute(
        array, AXIS, [(GROUP * p + i, GROUP * (p + way) + i) for p in froms for i in range(GROUP)]
    )


def hops(sends, step):
    return hop(sends[0], range(step), 1), hop(sends[1], range(PAIRS - step, PAIRS), -1)


def exchange(send):
    return lax.all_to_all(send, AXIS, 0, 0, axis_index_groups=NEAR, tiled=True)


def body(tokens, frozen_slot_rows, adapter_down_factor, adapter_up_factor, magnitude, counts):
    place = lax.axis_index(AXIS).astype(jnp.int32).reshape(1)
    own = own_windows(place, counts, tokens)
    moved = [to_pair(own[step], step) for step in range(1, PAIRS)]
    ups = [adapter_up_factor] + [to_pair(adapter_up_factor, step) for step in range(1, PAIRS)]
    column = collect(place, own, *moved, adapter_down_factor)
    other = lax.ppermute(column, AXIS, [(f, f ^ 4) for f in range(GROUP * PAIRS)])
    frozen_slot_rows, column = lax.optimization_barrier((frozen_slot_rows, column))
    sends = pack(place, frozen_slot_rows, PARTS[:1])
    sends[0], other = lax.optimization_barrier((sends[0], other))
    rows = exchange(sends[0])
    frozen_slot_rows, other = lax.optimization_barrier((frozen_slot_rows, other))
    sends += pack(place, frozen_slot_rows, PARTS[1:])
    blocks = jnp.stack([column, other])
    blocks = [blocks] + [along_x(blocks, step) for step in range(1, 4)]
    sends[1], rows, up1, up2, up3, *blocks = lax.optimization_barrier((sends[1], rows, *ups[1:], *blocks))
    all_tokens, down, up = assemble(place, blocks, [ups[0], up1, up2, up3])
    last_rows = exchange(sends[1])
    early_squares, early_front, early_back, first_front, first_back = partial_products(
        0, place, counts, rows, all_tokens, down, up
    )
    a, b = hops((first_front, first_front), 1), hops((first_back, first_back), 1)
    rows = last_rows
    a = hops(forward(2, place, a, early_front, early_front, early_squares, early_squares), 2)
    b = hops(forward(2, place, b, early_back, early_back, early_squares, early_squares), 2)
    rows, *a = lax.optimization_barrier((rows, *a))
    squares, front, back = partial_products(1, place, counts, rows, all_tokens, down, up)
    a = hops(forward(3, place, a, early_front, front, early_squares, squares), 3)
    b = hops(forward(3, place, b, early_back, back, early_squares, squares), 3)
    return finish(squares, magnitude.reshape(1, UNITS), front, back, [*a, *b])


def solution(mesh):
    in_specs = (
        P(("dp", "fsdp"), None),
        P(("dp", "fsdp"), None),
        P(("dp", "fsdp"), None),
        P("dp", "fsdp"),
        P(("dp", "fsdp")),
        P("dp"),
    )
    out_specs = P("dp", "fsdp")
    return jax.shard_map(body, mesh=mesh, in_specs=in_specs, out_specs=out_specs, check_vma=False)
```
